128 devices in a mesh: pair: 8 (over x, z_hi), ctr: 16 (over y, z_lo, core).
Axes of the slice: x: 4, y: 4, z: 4 (z_hi: 2, z_lo: 2; z = z_hi * 2 + z_lo), core: 2. Of those that a mesh axis runs over, the one named last changes fastest.
Arguments:
- amplitudes: bfloat16 [4096, 32768], P('pair', 'ctr'), may hold values from -6 to 6
- v_plus: bfloat16 [32768, 2048], P('ctr'), may hold values from -0.046875 to 0.046875
- v_minus: bfloat16 [32768, 2048], P('ctr'), may hold values from -0.046875 to 0.046875
- occ_irrep: int32 [64], replicated, may hold values from 0 to 7
- col_irrep: int32 [32768], P('ctr'), may hold values from 0 to 7
- block_map: int32 [8, 8], replicated, may hold values 0 or 1
Outputs:
- residual: bfloat16 [2048, 4096], P('ctr', 'pair')
The draws below stay inside these ranges and needn't reach their ends.
All inputs are finite; a program needn't handle non-finite values.
Results may differ from the reference program's by a relative error of at most 0.0052.
Values may be sent and summed in bfloat16 or wider, within the bound.
No kernel may reach another device: no remote copies, remote signals or barrier semaphores. Data moves between devices by JAX's collectives and lax.ppermute only.
A program may use at most 128 MiB of HBM per device.

```python
import jax
import jax.numpy as jnp
from jax import lax

NO = 64
NIRREP = 8
W = 2048
PAIRS = 4096
K = 32768


def touch_ends(array, rng, least, largest):
    index_at = [jax.random.randint(jax.random.fold_in(rng, axis), (), 0, length) for axis, length in enumerate(array.shape)]
    longest = array.shape.index(max(array.shape))
    next_to = index_at[:longest] + [(index_at[longest] + 1) % array.shape[longest]] + index_at[longest + 1:]
    return array.at[tuple(index_at)].set(least).at[tuple(next_to)].set(largest)


def raised(values, own_key, source, target, blocks, factor):
    def block_of(dim):
        return (jnp.arange(values.shape[dim]) // (values.shape[dim] // blocks)).reshape((-1,) + (1,) * (values.ndim - 1 - dim))

    first = jax.random.permutation(own_key, blocks)[block_of(target)]
    far = (block_of(target) + blocks // 2) % blocks
    return jnp.where((block_of(source) == first) | (block_of(source) == far), factor * values, values)


def levels(stream_key, extent, cuts, smallest, top_value):
    def one(position, parts):
        draws = jax.random.uniform(jax.random.fold_in(jax.random.fold_in(stream_key, 6), position), (parts,), jnp.float32, smallest / len(cuts), top_value / len(cuts))
        return jnp.repeat(jnp.exp(draws), extent[position] // parts).reshape((-1,) + (1,) * (len(extent) - position - 1))

    factor_of = one(*cuts[0])
    for cut in cuts[1:]:
        factor_of = factor_of * one(*cut)
    return factor_of


def normal_values(own_key, extent, width, limit, pieces=(), kind=jnp.bfloat16):
    drawn = jax.random.normal(own_key, extent, jnp.float32) * width
    if len(pieces) > 0:
        drawn = levels(own_key, extent, pieces, -0.22, 0.18) * drawn
    return jnp.clip(drawn, min=-limit, max=limit).astype(kind)


def bell_draw_with(key, extent, deviation, reach, cuts, heavy, dtype=jnp.bfloat16):
    array = deviation * jax.random.normal(key, extent, jnp.float32)
    if cuts:
        array = array * levels(key, extent, cuts, -0.22, 0.18)
    return jnp.clip(raised(array, jax.random.fold_in(key, 3), *heavy), -reach, reach).astype(dtype)


def setup_inputs(seed: int = 0) -> dict:
    splits = jax.random.split(jax.random.key(seed), 7)
    return {
        "amplitudes": normal_values(splits[0], (PAIRS, K), 1.0, 6.0, ((0, 8), (1, 16))),
        "v_plus": bell_draw_with(splits[1], (K, W), K ** -0.5, 0.046875, ((0, 16),), (0, 1, 16, 2.0)),
        "v_minus": bell_draw_with(splits[2], (K, W), K ** -0.5, 0.046875, ((0, 16),), (0, 1, 16, 2.0)),
        "occ_irrep": touch_ends(jax.random.randint(splits[3], (NO,), 0, NIRREP), jax.random.fold_in(splits[3], 1), 0, NIRREP - 1).astype(jnp.int32),
        "col_irrep": touch_ends(jax.random.randint(splits[4], (K,), 0, NIRREP), jax.random.fold_in(splits[4], 1), 0, NIRREP - 1).astype(jnp.int32),
        "block_map": touch_ends((jax.random.randint(splits[5], (NIRREP, NIRREP), 0, 2) < 1).astype(jnp.int32), jax.random.fold_in(splits[5], 1), 0, 1),
    }


def reference(amplitudes, v_plus, v_minus, occ_irrep, col_irrep, block_map):
    pair_irrep = jnp.bitwise_xor(occ_irrep[:, None], occ_irrep[None, :]).reshape(-1)
    keep = block_map[pair_irrep][:, col_irrep].astype(jnp.float32)
    depth = amplitudes.shape[1]
    orbitals = occ_irrep.shape[0]
    partner = amplitudes.reshape(orbitals, orbitals, depth).transpose(1, 0, 2).reshape(-1, depth)
    own_f = amplitudes.astype(jnp.float32)
    par_f = partner.astype(jnp.float32)
    sym = (keep * (own_f + par_f)).astype(jnp.bfloat16)
    anti = (keep * (own_f - par_f)).astype(jnp.bfloat16)
    dims = (((0,), (1,)), ((), ()))
    first = lax.dot_general(v_plus, sym, dims, preferred_element_type=jnp.float32)
    second = lax.dot_general(v_minus, anti, dims, preferred_element_type=jnp.float32)
    return (0.5 * (first + second)).astype(jnp.bfloat16)
```

```python
import functools

import jax
import jax.numpy as jnp
from jax import lax
from jax.experimental import pallas as pl
from jax.experimental.pallas import tpu as pltpu
from jax.sharding import Mesh, PartitionSpec as P

F32, BF16 = jnp.float32, jnp.bfloat16
LANES = 128
MIB = 1 << 20


def mask_rows(where_ref, occ_ref, map_ref, occ_col_ref, col_ref, t_ref, tm_ref):
    orbitals = occ_col_ref.shape[0]
    own = t_ref.shape[0] // orbitals
    irreps = map_ref.shape[0]
    kept = []
    for r in range(irreps):
        word = map_ref[r, 0]
        for c in range(1, irreps):
            word = word + map_ref[r, c] * (1 << c)
        kept.append(word)
    col = col_ref[...]
    for a in range(own):
        pair = occ_col_ref[...] ^ occ_ref[where_ref[0] * own + a]
        word = jnp.zeros_like(pair)
        for r in range(irreps):
            word = jnp.where(pair == r, kept[r], word)
        keep = jnp.right_shift(word, col) & 1
        rows = pl.ds(a * orbitals, orbitals)
        tm_ref[rows, :] = jnp.where(keep == 1, t_ref[rows, :].astype(F32), 0.0).astype(BF16)


def split_cores(core, acc, shape, keep_ref, send_ref, swap):
    low, high = acc[:, :LANES], acc[:, LANES:]
    mine = jnp.where(core == 0, low, high)
    other = jnp.where(core == 0, high, low)
    if swap:
        mine = jnp.swapaxes(mine.reshape(shape), 0, 1)
        other = jnp.swapaxes(other.reshape(shape), 0, 1)
    keep_ref[0] = mine.reshape(acc.shape[0], LANES)
    send_ref[0] = other.reshape(acc.shape[0], LANES).astype(BF16)


def v_kernel(where_ref, occ_ref, map_ref, occ_col_ref, col_ref, t_ref, p_ref, m_ref, keep_ref, send_ref, tm_ref):
    @pl.when(pl.program_id(0) == 0)
    def _():
        mask_rows(where_ref, occ_ref, map_ref, occ_col_ref, col_ref, t_ref, tm_ref)

    w = (p_ref[...].astype(F32) - m_ref[...].astype(F32)).astype(BF16)
    acc = jnp.dot(tm_ref[...], w, preferred_element_type=F32)
    own = t_ref.shape[0] // occ_col_ref.shape[0]
    shape = (own, occ_col_ref.shape[0] // own, own, LANES)
    split_cores(where_ref[1], acc, shape, keep_ref, send_ref, True)


def u_kernel(where_ref, tm_ref, p_ref, m_ref, keep_ref, send_ref):
    w = (p_ref[...].astype(F32) + m_ref[...].astype(F32)).astype(BF16)
    acc = jnp.dot(tm_ref[...], w, preferred_element_type=F32)
    split_cores(where_ref[1], acc, None, keep_ref, send_ref, False)


def last_kernel(own, u_ref, v_ref, out_ref, scratch):
    slabs, rows, _ = u_ref.shape
    u = u_ref[0].astype(F32)
    v = v_ref[0].astype(F32)
    for s in range(1, slabs):
        u = u + u_ref[s].astype(F32)
        v = v + v_ref[s].astype(F32)
    scratch[...] = v
    orbitals = rows // own
    parts = [scratch[pl.ds(b, orbitals, stride=own), :] for b in range(own)]
    total = 0.5 * (u + jnp.concatenate(parts, axis=0))
    out_ref[...] = total.T.astype(BF16)


def whole(shape):
    return pl.BlockSpec(shape, lambda s, *_: (0,) * len(shape))


def body(amplitudes, v_plus, v_minus, occ_irrep, col_irrep, block_map):
    rows, depth = amplitudes.shape
    width = v_plus.shape[1]
    orbitals = occ_irrep.shape[0]
    groups = lax.axis_size("x") * lax.axis_size("zh")
    own = orbitals // groups
    slabs = lax.axis_size("y") * lax.axis_size("zl")
    place = jnp.stack([lax.axis_index(("x", "zh")), lax.axis_index("c")]).astype(jnp.int32)
    half = [
        jax.ShapeDtypeStruct((slabs, rows, LANES), F32),
        jax.ShapeDtypeStruct((slabs, rows, LANES), BF16),
    ]
    masked = jax.ShapeDtypeStruct((rows, depth), BF16)
    half_specs = [pl.BlockSpec((1, rows, LANES), lambda s, *_: (s, 0, 0))] * 2
    slab_spec = pl.BlockSpec((depth, 2 * LANES), lambda s, *_: (0, s))
    smem = pl.BlockSpec(memory_space=pltpu.SMEM)
    params = pltpu.CompilerParams(vmem_limit_bytes=48 * MIB)
    cost = pl.CostEstimate(
        flops=2 * rows * depth * width, bytes_accessed=20 * MIB, transcendentals=0
    )
    v_keep, v_send, tm = pl.pallas_call(
        v_kernel,
        grid=(slabs,),
        in_specs=[smem, smem, smem, whole((orbitals, 1)), whole((1, depth)), whole((rows, depth)), slab_spec, slab_spec],
        out_specs=half_specs + [whole((rows, depth))],
        out_shape=half + [masked],
        compiler_params=params,
        cost_estimate=cost,
    )(place, occ_irrep, block_map, occ_irrep.reshape(orbitals, 1), col_irrep.reshape(1, depth), amplitudes, v_plus, v_minus)
    cores = [(0, 1), (1, 0)]
    v_got = lax.ppermute(v_send, "c", cores)
    v_part = (v_keep + v_got.astype(F32)).astype(BF16)
    v_all = lax.all_to_all(
        v_part.reshape(slabs * groups, rows // groups, LANES), ("y", "zl", "x", "zh"), 0, 0, tiled=True
    )

    u_keep, u_send = pl.pallas_call(
        u_kernel,
        grid=(slabs,),
        in_specs=[smem, whole((rows, depth)), slab_spec, slab_spec],
        out_specs=half_specs,
        out_shape=half,
        compiler_params=params,
        cost_estimate=cost,
    )(place, tm, v_plus, v_minus)
    u_got = lax.ppermute(u_send, "c", cores)
    u_part = (u_keep + u_got.astype(F32)).astype(BF16)
    u_all = lax.all_to_all(u_part, ("y", "zl"), 0, 0, tiled=True)

    return pl.pallas_call(
        functools.partial(last_kernel, own),
        out_shape=jax.ShapeDtypeStruct((LANES, rows), BF16),
        scratch_shapes=[pltpu.VMEM((rows, LANES), F32)],
        compiler_params=pltpu.CompilerParams(vmem_limit_bytes=24 * MIB),
    )(u_all, v_all.reshape(slabs, rows, LANES))


def solution(mesh):
    axes = ("x", "zh", "y", "zl", "c")
    fine = Mesh(mesh.devices.reshape(4, 2, 4, 2, 2), axes)
    pair, ctr = ("x", "zh"), ("y", "zl", "c")
    in_specs = (P(pair, ctr), P(ctr, None), P(ctr, None), P(), P(ctr), P())
    return jax.shard_map(body, mesh=fine, in_specs=in_specs, out_specs=P(ctr, pair), check_vma=False)
```

```python
import functools

import jax
import jax.numpy as jnp
from jax import lax
from jax.experimental import pallas as pl
from jax.experimental.pallas import tpu as pltpu
from jax.sharding import Mesh, PartitionSpec as P

F32, BF16, I32 = jnp.float32, jnp.bfloat16, jnp.int32
LANES = 128
MIB = 1 << 20


def across(column, width):
    return jnp.broadcast_to(column, (column.shape[0], width))


def mask_rows(me, occ_ref, map_ref, col_ref, t_ref, tm_ref, label_ref):
    orbitals = occ_ref.shape[1]
    rows, depth = t_ref.shape
    own = rows // orbitals
    irreps = map_ref.shape[0]
    square = (orbitals, orbitals)
    diagonal = lax.broadcasted_iota(I32, square, 0) == lax.broadcasted_iota(I32, square, 1)
    labels = jnp.where(diagonal, jnp.broadcast_to(occ_ref[...], square), 0)
    label_ref[...] = across(jnp.sum(labels, axis=1, keepdims=True), LANES)
    weights = jnp.left_shift(1, lax.broadcasted_iota(I32, map_ref.shape, 1))
    kept = across(jnp.sum(map_ref[...] * weights, axis=1, keepdims=True), LANES)
    col = col_ref[...]
    for a in range(own):
        pair = label_ref[...] ^ label_ref[pl.ds(me * own + a, 1), :]
        word = jnp.zeros_like(pair)
        for r in range(irreps):
            word = jnp.where(pair == r, kept[r : r + 1, :], word)
        word = jnp.concatenate([word] * (depth // LANES), axis=1)
        keep = jnp.right_shift(word, col) & 1
        part = pl.ds(a * orbitals, orbitals)
        tm_ref[part, :] = jnp.where(keep == 1, t_ref[part, :].astype(F32), 0.0).astype(BF16)


def main_kernel(
    occ_hbm, map_hbm, col_hbm, t_hbm, p_hbm, m_hbm,
    vk_hbm, vs_hbm, uk_hbm, us_hbm,
    occ_ref, map_ref, col_ref, label_ref, t_ref, tm_ref, p_ref, m_ref, vk_ref, vs_ref, uk_ref, us_ref,
    small_sem, p_sem, m_sem, out_sem,
):
    slabs = p_ref.shape[0]
    groups = vk_ref.shape[1]
    rows = t_ref.shape[0]
    own = vk_ref.shape[2] // groups
    me = lax.axis_index("x") * lax.axis_size("zh") + lax.axis_index("zh")
    y, zl, core = lax.axis_index("y"), lax.axis_index("zl"), lax.axis_index("c")

    small = [
        pltpu.make_async_copy(src, dst, small_sem.at[i])
        for i, (src, dst) in enumerate(((occ_hbm, occ_ref), (map_hbm, map_ref), (col_hbm, col_ref), (t_hbm, t_ref)))
    ]
    for copy in small:
        copy.start()

    def columns(s):
        return pl.ds(pl.multiple_of(s * 2 * LANES, 2 * LANES), 2 * LANES)

    def loads(s):
        return (
            pltpu.make_async_copy(p_hbm.at[:, columns(s)], p_ref.at[s], p_sem.at[s]),
            pltpu.make_async_copy(m_hbm.at[:, columns(s)], m_ref.at[s], m_sem.at[s]),
        )

    def start(s, carry):
        for copy in loads(s):
            copy.start()
        return carry

    lax.fori_loop(0, slabs, start, 0)
    for copy in small:
        copy.wait()
    mask_rows(me, occ_ref, map_ref, col_ref, t_ref, tm_ref, label_ref)

    half = rows // 2

    def stores(s):
        ys, zs = s // 2, s % 2
        z_slot = jnp.where(zs == zl, 0, 1)
        near, far = y ^ 1, 3 - y
        slot_a = jnp.where(ys == y, 0, jnp.where(ys == far, 1, jnp.where(ys == near, 2, 3)))
        slot_b = jnp.where(ys == y, 0, jnp.where(ys == near, 1, jnp.where(ys == far, 2, 3)))
        first, second = pl.ds(0, half), pl.ds(half, half)
        pairs = (
            (vk_ref.at[s], vk_hbm.at[:, s]),
            (vs_ref.at[s], vs_hbm.at[:, s]),
            (uk_ref.at[s, first], uk_hbm.at[0, slot_a, z_slot]),
            (uk_ref.at[s, second], uk_hbm.at[1, slot_b, z_slot]),
            (us_ref.at[s, first], us_hbm.at[0, slot_a, z_slot]),
            (us_ref.at[s, second], us_hbm.at[1, slot_b, z_slot]),
        )
        return [pltpu.make_async_copy(src, dst, out_sem.at[i, s]) for i, (src, dst) in enumerate(pairs)]

    def by_group(x):
        return jnp.swapaxes(x.reshape(own, groups, own, LANES), 0, 1).reshape(groups, own * own, LANES)

    def step(s, carry):
        for copy in loads(s):
            copy.wait()
        first = jnp.dot(tm_ref[...], p_ref[s], preferred_element_type=F32)
        second = jnp.dot(tm_ref[...], m_ref[s], preferred_element_type=F32)
        u, v = first + second, first - second
        u_low, u_high, v_low, v_high = u[:, :LANES], u[:, LANES:], v[:, :LANES], v[:, LANES:]
        uk_ref[s] = jnp.where(core == 0, u_low, u_high)
        us_ref[s] = jnp.where(core == 0, u_high, u_low).astype(BF16)
        vk_ref[s] = by_group(jnp.where(core == 0, v_low, v_high))
        vs_ref[s] = by_group(jnp.where(core == 0, v_high, v_low)).astype(BF16)
        for copy in stores(s):
            copy.start()
        return carry

    lax.fori_loop(0, slabs, step, 0)

    def finish(s, carry):
        for copy in stores(s):
            copy.wait()
        return carry

    lax.fori_loop(0, slabs, finish, 0)


def last_kernel(own, u_ref, got_ref, v_ref, out_ref, scratch):
    groups, slabs, block, _ = v_ref.shape
    for g in range(groups):
        v = v_ref[g, 0].astype(F32)
        for s in range(1, slabs):
            v = v + v_ref[g, s].astype(F32)
        scratch[pl.ds(g * block, block), :] = v
    orbitals = groups * own
    parts = [scratch[pl.ds(b, orbitals, stride=own), :] for b in range(own)]
    u = (u_ref[...] + got_ref[...].astype(F32)).reshape(groups * block, LANES)
    total = 0.5 * (u + jnp.concatenate(parts, axis=0))
    out_ref[...] = total.T.astype(BF16)


def body(amplitudes, v_plus, v_minus, occ_irrep, col_irrep, block_map):
    rows, depth = amplitudes.shape
    width = v_plus.shape[1]
    orbitals = occ_irrep.shape[0]
    groups = lax.axis_size("x") * lax.axis_size("zh")
    own = orbitals // groups
    ys, zs = lax.axis_size("y"), lax.axis_size("zl")
    slabs = ys * zs
    block = rows // groups
    anywhere = pl.BlockSpec(memory_space=pl.ANY)
    v_shape, u_shape = (groups, slabs, block, LANES), (2, ys, zs, rows // 2, LANES)
    v_keep, v_send, u_keep, u_send = pl.pallas_call(
        main_kernel,
        in_specs=[pl.BlockSpec(memory_space=pltpu.HBM)] * 6,
        out_specs=[anywhere] * 4,
        out_shape=[
            jax.ShapeDtypeStruct(v_shape, F32),
            jax.ShapeDtypeStruct(v_shape, BF16),
            jax.ShapeDtypeStruct(u_shape, F32),
            jax.ShapeDtypeStruct(u_shape, BF16),
        ],
        scratch_shapes=[
            pltpu.VMEM((1, orbitals), I32),
            pltpu.VMEM(block_map.shape, I32),
            pltpu.VMEM((1, depth), I32),
            pltpu.VMEM((orbitals, LANES), I32),
            pltpu.VMEM((rows, depth), BF16),
            pltpu.VMEM((rows, depth), BF16),
            pltpu.VMEM((slabs, depth, 2 * LANES), BF16),
            pltpu.VMEM((slabs, depth, 2 * LANES), BF16),
            pltpu.VMEM((slabs, groups, block, LANES), F32),
            pltpu.VMEM((slabs, groups, block, LANES), BF16),
            pltpu.VMEM((slabs, rows, LANES), F32),
            pltpu.VMEM((slabs, rows, LANES), BF16),
            pltpu.SemaphoreType.DMA((4,)),
            pltpu.SemaphoreType.DMA((slabs,)),
            pltpu.SemaphoreType.DMA((slabs,)),
            pltpu.SemaphoreType.DMA((6, slabs)),
        ],
        compiler_params=pltpu.CompilerParams(vmem_limit_bytes=44 * MIB),
        cost_estimate=pl.CostEstimate(flops=4 * rows * depth * width, bytes_accessed=24 * MIB, transcendentals=0),
    )(occ_irrep.reshape(1, orbitals), block_map, col_irrep.reshape(1, depth), amplitudes, v_plus, v_minus)

    cores = [(0, 1), (1, 0)]
    near = [(i, i ^ 1) for i in range(ys)]
    far = [(i, ys - 1 - i) for i in range(ys)]
    v_got = lax.ppermute(v_send, "c", cores)
    v_part = (v_keep + v_got.astype(F32)).astype(BF16)
    v_all = lax.all_to_all(
        v_part.reshape(groups * slabs, block, LANES), ("x", "zh", "y", "zl"), 0, 0, tiled=True
    )

    u_got = lax.ppermute(u_send, "c", cores)
    part = u_keep + u_got.astype(F32)
    out = part[:, 2:4].astype(BF16)
    got = jnp.stack([lax.ppermute(out[0], "y", near), lax.ppermute(out[1], "y", far)])
    part = part[:, 0:2] + got.astype(F32)
    out = part[:, 1].astype(BF16)
    got = jnp.stack([lax.ppermute(out[0], "y", far), lax.ppermute(out[1], "y", near)])
    part = part[:, 0] + got.astype(F32)
    u_last = lax.ppermute(part[:, 1].astype(BF16), "zl", cores)

    return pl.pallas_call(
        functools.partial(last_kernel, own),
        out_shape=jax.ShapeDtypeStruct((LANES, rows), BF16),
        scratch_shapes=[pltpu.VMEM((rows, LANES), F32)],
        compiler_params=pltpu.CompilerParams(vmem_limit_bytes=24 * MIB),
    )(part[:, 0], u_last, v_all.reshape(v_shape))


def solution(mesh):
    axes = ("x", "zh", "y", "zl", "c")
    fine = Mesh(mesh.devices.reshape(4, 2, 4, 2, 2), axes)
    pair, ctr = ("x", "zh"), ("y", "zl", "c")
    in_specs = (P(pair, ctr), P(ctr, None), P(ctr, None), P(), P(ctr), P())
    return jax.shard_map(body, mesh=fine, in_specs=in_specs, out_specs=P(ctr, pair), check_vma=False)
```

```python
import functools

import jax
import jax.numpy as jnp
from jax import lax
from jax.experimental import pallas as pl
from jax.experimental.pallas import tpu as pltpu
from jax.sharding import Mesh, PartitionSpec as P

F32, BF16, I32 = jnp.float32, jnp.bfloat16, jnp.int32
LANES = 128
MIB = 1 << 20


def across(column, width):
    return jnp.broadcast_to(column, (column.shape[0], width))


def mask_rows(me, occ_ref, map_ref, col_ref, t_ref, tm_ref, label_ref):
    orbitals = occ_ref.shape[1]
    rows, depth = t_ref.shape
    own = rows // orbitals
    irreps = map_ref.shape[0]
    square = (orbitals, orbitals)
    diagonal = lax.broadcasted_iota(I32, square, 0) == lax.broadcasted_iota(I32, square, 1)
    labels = jnp.where(diagonal, jnp.broadcast_to(occ_ref[...], square), 0)
    label_ref[...] = across(jnp.sum(labels, axis=1, keepdims=True), LANES)
    weights = jnp.left_shift(1, lax.broadcasted_iota(I32, map_ref.shape, 1))
    kept = across(jnp.sum(map_ref[...] * weights, axis=1, keepdims=True), LANES)
    col = col_ref[...]
    for a in range(own):
        pair = label_ref[...] ^ label_ref[pl.ds(me * own + a, 1), :]
        word = jnp.zeros_like(pair)
        for r in range(irreps):
            word = jnp.where(pair == r, kept[r : r + 1, :], word)
        word = jnp.concatenate([word] * (depth // LANES), axis=1)
        keep = jnp.right_shift(word, col) & 1
        part = pl.ds(a * orbitals, orbitals)
        tm_ref[part, :] = jnp.where(keep == 1, t_ref[part, :].astype(F32), 0.0).astype(BF16)


def main_kernel(
    occ_hbm, map_hbm, col_hbm, t_hbm, p_hbm, m_hbm,
    vk_ref, vs_ref, ua_ref, ub_ref, us_ref,
    occ_ref, map_ref, col_ref, label_ref, t_ref, tm_ref, p_ref, m_ref, small_sem, p_sem, m_sem,
):
    slabs = p_ref.shape[0]
    groups = vk_ref.shape[0]
    rows = t_ref.shape[0]
    half = rows // 2
    own = vk_ref.shape[2] // groups
    me = lax.axis_index("x") * lax.axis_size("zh") + lax.axis_index("zh")
    y, zl, core = lax.axis_index("y"), lax.axis_index("zl"), lax.axis_index("c")

    small = [
        pltpu.make_async_copy(src, dst, small_sem.at[i])
        for i, (src, dst) in enumerate(((occ_hbm, occ_ref), (map_hbm, map_ref), (col_hbm, col_ref), (t_hbm, t_ref)))
    ]
    for copy in small:
        copy.start()

    def columns(s):
        return pl.ds(pl.multiple_of(s * 2 * LANES, 2 * LANES), 2 * LANES)

    def loads(s):
        return (
            pltpu.make_async_copy(p_hbm.at[:, columns(s)], p_ref.at[s], p_sem.at[s]),
            pltpu.make_async_copy(m_hbm.at[:, columns(s)], m_ref.at[s], m_sem.at[s]),
        )

    def start(s, carry):
        for copy in loads(s):
            copy.start()
        return carry

    lax.fori_loop(0, slabs, start, 0)
    for copy in small:
        copy.wait()
    mask_rows(me, occ_ref, map_ref, col_ref, t_ref, tm_ref, label_ref)

    def by_group(x):
        return jnp.swapaxes(x.reshape(own, groups, own, LANES), 0, 1).reshape(groups, own * own, LANES)

    near, far = y ^ 1, 3 - y

    def step(s, carry):
        for copy in loads(s):
            copy.wait()
        first = jnp.dot(tm_ref[...], p_ref[s], preferred_element_type=F32)
        second = jnp.dot(tm_ref[...], m_ref[s], preferred_element_type=F32)
        u, v = first + second, first - second
        u_low, u_high, v_low, v_high = u[:, :LANES], u[:, LANES:], v[:, :LANES], v[:, LANES:]
        vk_ref[:, s] = by_group(jnp.where(core == 0, v_low, v_high))
        vs_ref[:, s] = by_group(jnp.where(core == 0, v_high, v_low)).astype(BF16)
        ys, zs = s // 2, s % 2
        z_slot = jnp.where(zs == zl, 0, 1)
        slot_a = jnp.where(ys == y, 0, jnp.where(ys == far, 1, jnp.where(ys == near, 2, 3)))
        slot_b = jnp.where(ys == y, 0, jnp.where(ys == near, 1, jnp.where(ys == far, 2, 3)))
        u_keep = jnp.where(core == 0, u_low, u_high)
        u_send = jnp.where(core == 0, u_high, u_low).astype(BF16)
        ua_ref[slot_a, z_slot] = u_keep[:half]
        ub_ref[slot_b, z_slot] = u_keep[half:]
        us_ref[0, slot_a, z_slot] = u_send[:half]
        us_ref[1, slot_b, z_slot] = u_send[half:]
        return carry

    lax.fori_loop(0, slabs, step, 0)


def last_kernel(own, *refs):
    *u_refs, v_ref, out_ref, scratch = refs
    groups, slabs, block, _ = v_ref.shape
    for g in range(groups):
        v = v_ref[g, 0].astype(F32)
        for s in range(1, slabs):
            v = v + v_ref[g, s].astype(F32)
        scratch[pl.ds(g * block, block), :] = v
    orbitals = groups * own
    parts = [scratch[pl.ds(b, orbitals, stride=own), :] for b in range(own)]
    count = len(u_refs) // 2
    halves = []
    for refs in (u_refs[:count], u_refs[count:]):
        u = refs[0][...].astype(F32)
        for ref in refs[1:]:
            u = u + ref[...].astype(F32)
        halves.append(u)
    total = 0.5 * (jnp.concatenate(halves, axis=0) + jnp.concatenate(parts, axis=0))
    out_ref[...] = total.T.astype(BF16)


def body(amplitudes, v_plus, v_minus, occ_irrep, col_irrep, block_map):
    rows, depth = amplitudes.shape
    width = v_plus.shape[1]
    orbitals = occ_irrep.shape[0]
    groups = lax.axis_size("x") * lax.axis_size("zh")
    own = orbitals // groups
    ys, zs = lax.axis_size("y"), lax.axis_size("zl")
    slabs = ys * zs
    block = rows // groups
    in_vmem = pl.BlockSpec(memory_space=pltpu.VMEM)
    operands = (occ_irrep.reshape(1, orbitals), block_map, col_irrep.reshape(1, depth), amplitudes, v_plus, v_minus)
    v_shape, u_shape = (groups, slabs, block, LANES), (ys, zs, rows // 2, LANES)
    v_keep, v_send, a_keep, b_keep, u_send = pl.pallas_call(
        main_kernel,
        in_specs=[pl.BlockSpec(memory_space=pltpu.HBM)] * 6,
        out_specs=[in_vmem] * 5,
        out_shape=[
            pltpu.VMEM(v_shape, F32),
            pltpu.VMEM(v_shape, BF16),
            pltpu.VMEM(u_shape, F32),
            pltpu.VMEM(u_shape, F32),
            pltpu.VMEM((2,) + u_shape, BF16),
        ],
        scratch_shapes=[
            pltpu.VMEM((1, orbitals), I32),
            pltpu.VMEM(block_map.shape, I32),
            pltpu.VMEM((1, depth), I32),
            pltpu.VMEM((orbitals, LANES), I32),
            pltpu.VMEM((rows, depth), BF16),
            pltpu.VMEM((rows, depth), BF16),
            pltpu.VMEM((slabs, depth, 2 * LANES), BF16),
            pltpu.VMEM((slabs, depth, 2 * LANES), BF16),
            pltpu.SemaphoreType.DMA((4,)),
            pltpu.SemaphoreType.DMA((slabs,)),
            pltpu.SemaphoreType.DMA((slabs,)),
        ],
        compiler_params=pltpu.CompilerParams(vmem_limit_bytes=40 * MIB),
        cost_estimate=pl.CostEstimate(flops=4 * rows * depth * width, bytes_accessed=24 * MIB, transcendentals=0),
    )(*(pltpu.with_memory_space_constraint(x, pltpu.HBM) for x in operands))

    cores = [(0, 1), (1, 0)]
    near = [(i, i ^ 1) for i in range(ys)]
    far = [(i, ys - 1 - i) for i in range(ys)]
    near_z = [(2 * a + z, 2 * b + 1 - z) for a, b in near for z in range(2)]
    far_z = [(2 * a + z, 2 * b + 1 - z) for a, b in far for z in range(2)]
    yz = ("y", "zl")
    u_got = lax.ppermute(u_send, "c", cores)
    v_got = lax.ppermute(v_send, "c", cores)
    a_all = a_keep + u_got[0].astype(F32)
    b_all = b_keep + u_got[1].astype(F32)
    a_got = lax.ppermute(a_all[2:4].astype(BF16), "y", near)
    b_got = lax.ppermute(b_all[2:4].astype(BF16), "y", far)
    v_part = (v_keep + v_got.astype(F32)).astype(BF16)
    v_all = lax.all_to_all(
        v_part.reshape(groups * slabs, block, LANES), ("x", "zh", "y", "zl"), 0, 0, tiled=True
    )
    terms = []
    for all_, got, one, two in ((a_all, a_got, far, far_z), (b_all, b_got, near, near_z)):
        part = all_[0:2] + got.astype(F32)
        sends = part.astype(BF16)
        terms += [
            part[0, 0],
            lax.ppermute(sends[1, 0], "y", one),
            lax.ppermute(sends[0, 1], "zl", cores),
            lax.ppermute(sends[1, 1], yz, two),
        ]

    return pl.pallas_call(
        functools.partial(last_kernel, own),
        out_shape=jax.ShapeDtypeStruct((LANES, rows), BF16),
        scratch_shapes=[pltpu.VMEM((rows, LANES), F32)],
        compiler_params=pltpu.CompilerParams(vmem_limit_bytes=24 * MIB),
    )(*terms, v_all.reshape(v_shape))


def solution(mesh):
    axes = ("x", "zh", "y", "zl", "c")
    fine = Mesh(mesh.devices.reshape(4, 2, 4, 2, 2), axes)
    pair, ctr = ("x", "zh"), ("y", "zl", "c")
    in_specs = (P(pair, ctr), P(ctr, None), P(ctr, None), P(), P(ctr), P())
    return jax.shard_map(body, mesh=fine, in_specs=in_specs, out_specs=P(ctr, pair), check_vma=False)
```

```python
import functools

import jax
import jax.numpy as jnp
from jax import lax
from jax.experimental import pallas as pl
from jax.experimental.pallas import tpu as pltpu
from jax.sharding import Mesh, PartitionSpec as P

F32, BF16, I32, I16 = jnp.float32, jnp.bfloat16, jnp.int32, jnp.int16
LANES = 128
MIB = 1 << 20
VMEM = pl.BlockSpec(memory_space=pltpu.VMEM)
HBM = pl.BlockSpec(memory_space=pltpu.HBM)


def across(column, width):
    return jnp.broadcast_to(column, (column.shape[0], width))


def mask_rows(me, occ_ref, map_ref, col_ref, t_ref, tm_ref, label_ref):
    orbitals = occ_ref.shape[1]
    rows, depth = t_ref.shape
    own = rows // orbitals
    irreps = map_ref.shape[0]
    square = (orbitals, orbitals)
    diagonal = lax.broadcasted_iota(I32, square, 0) == lax.broadcasted_iota(I32, square, 1)
    labels = jnp.where(diagonal, jnp.broadcast_to(occ_ref[...], square), 0)
    label_ref[...] = across(jnp.sum(labels, axis=1, keepdims=True), LANES)
    weights = jnp.left_shift(1, lax.broadcasted_iota(I32, map_ref.shape, 1))
    kept = across(jnp.sum(map_ref[...] * weights, axis=1, keepdims=True), LANES)
    bit = jnp.left_shift(1, jnp.broadcast_to(col_ref[...], (16, depth))).astype(I16)
    bit = jnp.concatenate([bit] * (orbitals // 16), axis=0)
    for a in range(own):
        pair = label_ref[...] ^ label_ref[pl.ds(me * own + a, 1), :]
        word = jnp.zeros_like(pair)
        for r in range(irreps):
            word = jnp.where(pair == r, kept[r : r + 1, :], word)
        word = jnp.concatenate([word.astype(I16)] * (depth // LANES), axis=1)
        part = pl.ds(a * orbitals, orbitals)
        tm_ref[part, :] = jnp.where((word & bit) != 0, t_ref[part, :], jnp.zeros((), BF16))


def by_group(x, shape):
    groups, block, _ = shape
    own = block // groups
    return jnp.swapaxes(x.reshape(own, groups, own, LANES), 0, 1).reshape(shape)


def v_kernel(
    occ_hbm, map_hbm, col_hbm, t_hbm, p_hbm, m_hbm,
    keep_ref, send_ref, tm_ref, p_ref, m_ref,
    occ_ref, map_ref, col_ref, label_ref, t_ref, small_sem, p_sem, m_sem,
):
    slabs = p_ref.shape[0]
    groups, _, block, _ = keep_ref.shape
    wide = 2 * LANES
    me = lax.axis_index("x") * lax.axis_size("zh") + lax.axis_index("zh")
    core = lax.axis_index("c")
    small = [
        pltpu.make_async_copy(src, dst, small_sem.at[i])
        for i, (src, dst) in enumerate(((t_hbm, t_ref), (occ_hbm, occ_ref), (map_hbm, map_ref), (col_hbm, col_ref)))
    ]
    for copy in small:
        copy.start()

    def loads(s):
        columns = pl.ds(pl.multiple_of(s * wide, wide), wide)
        return (
            pltpu.make_async_copy(p_hbm.at[:, columns], p_ref.at[s], p_sem.at[s]),
            pltpu.make_async_copy(m_hbm.at[:, columns], m_ref.at[s], m_sem.at[s]),
        )

    def start(s, carry):
        for copy in loads(s):
            copy.start()
        return carry

    lax.fori_loop(0, slabs, start, 0)
    for copy in small:
        copy.wait()
    mask_rows(me, occ_ref, map_ref, col_ref, t_ref, tm_ref, label_ref)
    shape = (groups, block, LANES)

    def step(b, carry):
        weights = []
        for i in range(2):
            for copy in loads(2 * b + i):
                copy.wait()
            weights.append(p_ref[2 * b + i] - m_ref[2 * b + i])
        v = jnp.dot(tm_ref[...], jnp.concatenate(weights, axis=1), preferred_element_type=F32)
        for i in range(2):
            low = v[:, 2 * i * LANES : (2 * i + 1) * LANES]
            high = v[:, (2 * i + 1) * LANES : (2 * i + 2) * LANES]
            keep_ref[:, 2 * b + i] = by_group(jnp.where(core == 0, low, high), shape)
            send_ref[:, 2 * b + i] = by_group(jnp.where(core == 0, high, low), shape).astype(BF16)
        return carry

    lax.fori_loop(0, slabs // 2, step, 0)


def u_kernel(other, tm_ref, p_ref, m_ref, out_ref):
    y, zl, core = lax.axis_index("y"), lax.axis_index("zl"), lax.axis_index("c")
    parity = 1 - core if other else core
    columns = pl.ds(pl.multiple_of(parity * LANES, LANES), LANES)
    near, far = y ^ 1, 3 - y

    def step(b, carry):
        weights = [p_ref[4 * b + i, :, columns] + m_ref[4 * b + i, :, columns] for i in range(4)]
        u = jnp.dot(tm_ref[...], jnp.concatenate(weights, axis=1), preferred_element_type=F32)
        for i in range(4):
            s = 4 * b + i
            ys, zs = s // 2, s % 2
            z_slot = jnp.where(zs == zl, 0, 1)
            y_slot = jnp.where(ys == y, 0, jnp.where(ys == far, 1, jnp.where(ys == near, 2, 3)))
            out_ref[y_slot, z_slot] = u[:, i * LANES : (i + 1) * LANES].astype(out_ref.dtype)
        return carry

    lax.fori_loop(0, p_ref.shape[0] // 4, step, 0)


def v_add_kernel(keep_ref, got_ref, out_ref):
    def step(h, carry):
        out_ref[h] = (keep_ref[h] + got_ref[h].astype(F32)).astype(BF16)
        return carry

    lax.fori_loop(0, out_ref.shape[0], step, 0)


def first_add_kernel(keep_ref, got_ref, out_ref, rest_ref):
    for slot in range(2):
        for z in range(2):
            total = keep_ref[2 + slot, z] + got_ref[2 + slot, z].astype(F32)
            out_ref[slot, z] = total.astype(BF16)
            rest_ref[slot, z] = keep_ref[slot, z] + got_ref[slot, z].astype(F32)


def second_add_kernel(rest_ref, more_ref, mine_ref, *out_refs):
    for ref, (slot, z) in zip((mine_ref, *out_refs), ((0, 0), (1, 1), (1, 0), (0, 1))):
        ref[...] = (rest_ref[slot, z] + more_ref[slot, z].astype(F32)).astype(ref.dtype)


def last_kernel(mine_ref, far_ref, z_ref, both_ref, v_ref, out_ref, scratch):
    groups, slabs, block, _ = v_ref.shape
    own = block // groups
    for g in range(groups):
        v = v_ref[g, 0].astype(F32)
        for s in range(1, slabs):
            v = v + v_ref[g, s].astype(F32)
        scratch[pl.ds(g * block, block), :] = v
    orbitals = groups * own
    parts = [scratch[pl.ds(b, orbitals, stride=own), :] for b in range(own)]
    u = mine_ref[...]
    for ref in (far_ref, z_ref, both_ref):
        u = u + ref[...].astype(F32)
    out_ref[...] = (0.5 * (u + jnp.concatenate(parts, axis=0))).T.astype(BF16)


def held(x):
    return pltpu.with_memory_space_constraint(x, pltpu.VMEM)


def call(kernel, out_shape, *operands, flops=MIB, scratch=()):
    return pl.pallas_call(
        kernel,
        in_specs=[VMEM] * len(operands),
        out_specs=jax.tree.map(lambda _: VMEM, out_shape),
        out_shape=out_shape,
        scratch_shapes=scratch,
        compiler_params=pltpu.CompilerParams(vmem_limit_bytes=8 * MIB),
        cost_estimate=pl.CostEstimate(flops=flops, bytes_accessed=4 * MIB, transcendentals=0),
    )(*operands)


def body(amplitudes, v_plus, v_minus, occ_irrep, col_irrep, block_map):
    rows, depth = amplitudes.shape
    width = v_plus.shape[1]
    orbitals = occ_irrep.shape[0]
    groups = lax.axis_size("x") * lax.axis_size("zh")
    ys, zs = lax.axis_size("y"), lax.axis_size("zl")
    slabs = ys * zs
    block = rows // groups
    operands = (occ_irrep.reshape(1, orbitals), block_map, col_irrep.reshape(1, depth), amplitudes, v_plus, v_minus)
    v_shape, u_shape = (groups, slabs, block, LANES), (ys, zs, rows, LANES)
    wide = (slabs, depth, 2 * LANES)
    flops = rows * depth * width
    v_keep, v_send, tm, p, m = pl.pallas_call(
        v_kernel,
        in_specs=[HBM] * 6,
        out_specs=[VMEM] * 5,
        out_shape=[
            pltpu.VMEM(v_shape, F32),
            pltpu.VMEM(v_shape, BF16),
            pltpu.VMEM((rows, depth), BF16),
            pltpu.VMEM(wide, BF16),
            pltpu.VMEM(wide, BF16),
        ],
        scratch_shapes=[
            pltpu.VMEM((1, orbitals), I32),
            pltpu.VMEM(block_map.shape, I32),
            pltpu.VMEM((1, depth), I32),
            pltpu.VMEM((orbitals, LANES), I32),
            pltpu.VMEM((rows, depth), BF16),
            pltpu.SemaphoreType.DMA((4,)),
            pltpu.SemaphoreType.DMA((slabs,)),
            pltpu.SemaphoreType.DMA((slabs,)),
        ],
        compiler_params=pltpu.CompilerParams(vmem_limit_bytes=12 * MIB),
        cost_estimate=pl.CostEstimate(flops=2 * flops, bytes_accessed=20 * MIB, transcendentals=0),
    )(*(pltpu.with_memory_space_constraint(x, pltpu.HBM) for x in operands))

    def after(x, *others):
        return lax.optimization_barrier((x, *others))[0]

    cores = [(0, 1), (1, 0)]
    near = [(i, i ^ 1) for i in range(ys)]
    far = [(i, ys - 1 - i) for i in range(ys)]
    far_z = [(2 * a + z, 2 * b + 1 - z) for a, b in far for z in range(2)]
    flat = (rows, LANES)
    v_got = lax.ppermute(v_send, "c", cores)
    u_send = call(functools.partial(u_kernel, True), pltpu.VMEM(u_shape, BF16), held(tm), held(p), held(m), flops=flops)
    v_keep = after(v_keep, u_send)
    v_part = call(v_add_kernel, jax.ShapeDtypeStruct(v_shape, BF16), held(v_keep), held(v_got))
    u_got = lax.ppermute(u_send, "c", cores)
    tm = after(tm, v_part)
    u_keep = call(functools.partial(u_kernel, False), pltpu.VMEM(u_shape, F32), held(tm), held(p), held(m), flops=flops)
    u_out, rest = call(
        first_add_kernel,
        [jax.ShapeDtypeStruct((2, zs, *flat), BF16), pltpu.VMEM((2, zs, *flat), F32)],
        held(u_keep), held(u_got),
    )
    u_more = lax.ppermute(u_out, "y", near)
    v_part = after(v_part, rest)
    v_all = lax.all_to_all(
        v_part.reshape(groups * slabs, block, LANES), ("x", "zh", "y", "zl"), 0, 0, tiled=True
    )
    mine, to_both, to_far, to_z = call(
        second_add_kernel,
        [pltpu.VMEM(flat, F32)] + [jax.ShapeDtypeStruct(flat, BF16)] * 3,
        held(rest), u_more, flops=40 << 30,
    )
    return call(
        last_kernel,
        jax.ShapeDtypeStruct((LANES, rows), BF16),
        mine,
        lax.ppermute(to_both, ("y", "zl"), far_z),
        lax.ppermute(to_far, "y", far),
        lax.ppermute(to_z, "zl", cores),
        v_all.reshape(v_shape),
        scratch=[pltpu.VMEM(flat, F32)],
    )


def solution(mesh):
    axes = ("x", "zh", "y", "zl", "c")
    fine = Mesh(mesh.devices.reshape(4, 2, 4, 2, 2), axes)
    pair, ctr = ("x", "zh"), ("y", "zl", "c")
    in_specs = (P(pair, ctr), P(ctr, None), P(ctr, None), P(), P(ctr), P())
    return jax.shard_map(body, mesh=fine, in_specs=in_specs, out_specs=P(ctr, pair), check_vma=False)
```

```python
import functools

import jax
import jax.numpy as jnp
from jax import lax
from jax.experimental import pallas as pl
from jax.experimental.pallas import tpu as pltpu
from jax.sharding import Mesh, PartitionSpec as P

F32, BF16, I32, I16 = jnp.float32, jnp.bfloat16, jnp.int32, jnp.int16
LANES = 128
MIB = 1 << 20
VMEM = pl.BlockSpec(memory_space=pltpu.VMEM)
HBM = pl.BlockSpec(memory_space=pltpu.HBM)


def across(column, width):
    return jnp.broadcast_to(column, (column.shape[0], width))


def mask_rows(me, occ_ref, map_ref, col_ref, t_ref, tm_ref, label_ref):
    orbitals = occ_ref.shape[1]
    rows, depth = t_ref.shape
    own = rows // orbitals
    irreps = map_ref.shape[0]
    square = (orbitals, orbitals)
    diagonal = lax.broadcasted_iota(I32, square, 0) == lax.broadcasted_iota(I32, square, 1)
    labels = jnp.where(diagonal, jnp.broadcast_to(occ_ref[...], square), 0)
    label_ref[...] = across(jnp.sum(labels, axis=1, keepdims=True), LANES)
    weights = jnp.left_shift(1, lax.broadcasted_iota(I32, map_ref.shape, 1))
    kept = across(jnp.sum(map_ref[...] * weights, axis=1, keepdims=True), LANES)
    bit = jnp.left_shift(1, jnp.broadcast_to(col_ref[...], (16, depth))).astype(I16)
    bit = jnp.concatenate([bit] * (orbitals // 16), axis=0)
    for a in range(own):
        pair = label_ref[...] ^ label_ref[pl.ds(me * own + a, 1), :]
        word = jnp.zeros_like(pair)
        for r in range(irreps):
            word = jnp.where(pair == r, kept[r : r + 1, :], word)
        word = jnp.concatenate([word.astype(I16)] * (depth // LANES), axis=1)
        part = pl.ds(a * orbitals, orbitals)
        tm_ref[part, :] = jnp.where((word & bit) != 0, t_ref[part, :], jnp.zeros((), BF16))


def by_group(x, shape):
    groups, block, _ = shape
    own = block // groups
    return jnp.swapaxes(x.reshape(own, groups, own, LANES), 0, 1).reshape(shape)


def v_kernel(
    occ_hbm, map_hbm, col_hbm, t_hbm, p_hbm, m_hbm,
    keep_ref, send_ref, tm_ref, p_ref, m_ref,
    occ_ref, map_ref, col_ref, label_ref, t_ref, small_sem, p_sem, m_sem,
):
    slabs = p_ref.shape[0]
    groups, _, block, _ = keep_ref.shape
    wide = 2 * LANES
    me = lax.axis_index("x") * lax.axis_size("zh") + lax.axis_index("zh")
    core = lax.axis_index("c")
    small = [
        pltpu.make_async_copy(src, dst, small_sem.at[i])
        for i, (src, dst) in enumerate(((t_hbm, t_ref), (occ_hbm, occ_ref), (map_hbm, map_ref), (col_hbm, col_ref)))
    ]
    for copy in small:
        copy.start()

    def loads(s):
        columns = pl.ds(pl.multiple_of(s * wide, wide), wide)
        return (
            pltpu.make_async_copy(p_hbm.at[:, columns], p_ref.at[s], p_sem.at[s]),
            pltpu.make_async_copy(m_hbm.at[:, columns], m_ref.at[s], m_sem.at[s]),
        )

    def start(s, carry):
        for copy in loads(s):
            copy.start()
        return carry

    lax.fori_loop(0, slabs, start, 0)
    for copy in small:
        copy.wait()
    mask_rows(me, occ_ref, map_ref, col_ref, t_ref, tm_ref, label_ref)
    shape = (groups, block, LANES)

    def step(b, carry):
        weights = []
        for i in range(2):
            for copy in loads(2 * b + i):
                copy.wait()
            weights.append(p_ref[2 * b + i] - m_ref[2 * b + i])
        v = jnp.dot(tm_ref[...], jnp.concatenate(weights, axis=1), preferred_element_type=F32)
        for i in range(2):
            low = v[:, 2 * i * LANES : (2 * i + 1) * LANES]
            high = v[:, (2 * i + 1) * LANES : (2 * i + 2) * LANES]
            keep_ref[:, 2 * b + i] = by_group(jnp.where(core == 0, low, high), shape)
            send_ref[:, 2 * b + i] = by_group(jnp.where(core == 0, high, low), shape).astype(BF16)
        return carry

    lax.fori_loop(0, slabs // 2, step, 0)


def u_kernel(parity, tm_ref, p_ref, m_ref, out_ref):
    y, zl = lax.axis_index("y"), lax.axis_index("zl")
    columns = pl.ds(pl.multiple_of(parity * LANES, LANES), LANES)
    near, far = y ^ 1, 3 - y

    def step(b, carry):
        weights = [p_ref[4 * b + i, :, columns] + m_ref[4 * b + i, :, columns] for i in range(4)]
        u = jnp.dot(tm_ref[...], jnp.concatenate(weights, axis=1), preferred_element_type=F32)
        for i in range(4):
            s = 4 * b + i
            ys, zs = s // 2, s % 2
            z_slot = jnp.where(zs == zl, 0, 1)
            y_slot = jnp.where(ys == y, 0, jnp.where(ys == far, 1, jnp.where(ys == near, 2, 3)))
            out_ref[y_slot, z_slot] = u[:, i * LANES : (i + 1) * LANES].astype(out_ref.dtype)
        return carry

    lax.fori_loop(0, p_ref.shape[0] // 4, step, 0)


def u_send_kernel(*refs):
    u_kernel(1 - lax.axis_index("c"), *refs)


def u_keep_kernel(tm_ref, p_ref, m_ref, vk_ref, vg_ref, out_ref, v_hbm, v_ref, sem):
    copies = []
    for h in range(v_ref.shape[0]):
        v_ref[h] = (vk_ref[h] + vg_ref[h].astype(F32)).astype(BF16)
        copies.append(pltpu.make_async_copy(v_ref.at[h], v_hbm.at[h], sem.at[h]))
        copies[-1].start()
    u_kernel(lax.axis_index("c"), tm_ref, p_ref, m_ref, out_ref)
    for copy in copies:
        copy.wait()


def first_add_kernel(keep_ref, got_ref, out_ref, rest_ref):
    for slot in range(2):
        for z in range(2):
            total = keep_ref[2 + slot, z] + got_ref[2 + slot, z].astype(F32)
            out_ref[slot, z] = total.astype(BF16)
            rest_ref[slot, z] = keep_ref[slot, z] + got_ref[slot, z].astype(F32)


def second_add_kernel(rest_ref, more_ref, mine_ref, *out_refs):
    for ref, (slot, z) in zip((mine_ref, *out_refs), ((0, 0), (1, 1), (1, 0), (0, 1))):
        ref[...] = (rest_ref[slot, z] + more_ref[slot, z].astype(F32)).astype(ref.dtype)


def last_kernel(mine_ref, far_ref, z_ref, both_ref, v_ref, out_ref, scratch):
    groups, slabs, block, _ = v_ref.shape
    own = block // groups
    for g in range(groups):
        v = v_ref[g, 0].astype(F32)
        for s in range(1, slabs):
            v = v + v_ref[g, s].astype(F32)
        scratch[pl.ds(g * block, block), :] = v
    orbitals = groups * own
    parts = [scratch[pl.ds(b, orbitals, stride=own), :] for b in range(own)]
    u = mine_ref[...]
    for ref in (far_ref, z_ref, both_ref):
        u = u + ref[...].astype(F32)
    out_ref[...] = (0.5 * (u + jnp.concatenate(parts, axis=0))).T.astype(BF16)


def held(x):
    return pltpu.with_memory_space_constraint(x, pltpu.VMEM)


def call(kernel, out_shape, *operands, flops=MIB, scratch=()):
    return pl.pallas_call(
        kernel,
        in_specs=[VMEM] * len(operands),
        out_specs=jax.tree.map(lambda _: VMEM, out_shape),
        out_shape=out_shape,
        scratch_shapes=scratch,
        compiler_params=pltpu.CompilerParams(vmem_limit_bytes=8 * MIB),
        cost_estimate=pl.CostEstimate(flops=flops, bytes_accessed=4 * MIB, transcendentals=0),
    )(*operands)


def body(amplitudes, v_plus, v_minus, occ_irrep, col_irrep, block_map):
    rows, depth = amplitudes.shape
    width = v_plus.shape[1]
    orbitals = occ_irrep.shape[0]
    groups = lax.axis_size("x") * lax.axis_size("zh")
    ys, zs = lax.axis_size("y"), lax.axis_size("zl")
    slabs = ys * zs
    block = rows // groups
    operands = (occ_irrep.reshape(1, orbitals), block_map, col_irrep.reshape(1, depth), amplitudes, v_plus, v_minus)
    v_shape, u_shape = (groups, slabs, block, LANES), (ys, zs, rows, LANES)
    wide = (slabs, depth, 2 * LANES)
    flops = rows * depth * width
    v_keep, v_send, tm, p, m = pl.pallas_call(
        v_kernel,
        in_specs=[HBM] * 6,
        out_specs=[VMEM] * 5,
        out_shape=[
            pltpu.VMEM(v_shape, F32),
            pltpu.VMEM(v_shape, BF16),
            pltpu.VMEM((rows, depth), BF16),
            pltpu.VMEM(wide, BF16),
            pltpu.VMEM(wide, BF16),
        ],
        scratch_shapes=[
            pltpu.VMEM((1, orbitals), I32),
            pltpu.VMEM(block_map.shape, I32),
            pltpu.VMEM((1, depth), I32),
            pltpu.VMEM((orbitals, LANES), I32),
            pltpu.VMEM((rows, depth), BF16),
            pltpu.SemaphoreType.DMA((4,)),
            pltpu.SemaphoreType.DMA((slabs,)),
            pltpu.SemaphoreType.DMA((slabs,)),
        ],
        compiler_params=pltpu.CompilerParams(vmem_limit_bytes=12 * MIB),
        cost_estimate=pl.CostEstimate(flops=2 * flops, bytes_accessed=20 * MIB, transcendentals=0),
    )(*(pltpu.with_memory_space_constraint(x, pltpu.HBM) for x in operands))

    def after(x, *others):
        return lax.optimization_barrier((x, *others))[0]

    cores = [(0, 1), (1, 0)]
    near = [(i, i ^ 1) for i in range(ys)]
    far = [(i, ys - 1 - i) for i in range(ys)]
    far_z = [(2 * a + z, 2 * b + 1 - z) for a, b in far for z in range(2)]
    flat = (rows, LANES)
    v_got = lax.ppermute(v_send, "c", cores)
    factors = [held(x) for x in (tm, p, m)]
    u_send = call(u_send_kernel, pltpu.VMEM(u_shape, BF16), *factors, flops=flops)
    u_got = lax.ppermute(u_send, "c", cores)
    u_keep, v_part = pl.pallas_call(
        u_keep_kernel,
        in_specs=[VMEM] * 5,
        out_specs=[VMEM, HBM],
        out_shape=[pltpu.VMEM(u_shape, F32), pltpu.HBM(v_shape, BF16)],
        scratch_shapes=[pltpu.VMEM(v_shape, BF16), pltpu.SemaphoreType.DMA((groups,))],
        compiler_params=pltpu.CompilerParams(vmem_limit_bytes=8 * MIB),
        cost_estimate=pl.CostEstimate(flops=flops, bytes_accessed=4 * MIB, transcendentals=0),
    )(*factors, held(after(v_keep, u_send)), held(v_got))
    u_out, rest = call(
        first_add_kernel,
        [jax.ShapeDtypeStruct((2, zs, *flat), BF16), pltpu.VMEM((2, zs, *flat), F32)],
        held(u_keep), held(u_got),
    )
    u_more = lax.ppermute(u_out, "y", near)
    v_part = after(v_part, rest)
    v_all = lax.all_to_all(
        v_part.reshape(groups * slabs, block, LANES), ("x", "zh", "y", "zl"), 0, 0, tiled=True
    )
    mine, to_both, to_far, to_z = call(
        second_add_kernel,
        [pltpu.VMEM(flat, F32)] + [jax.ShapeDtypeStruct(flat, BF16)] * 3,
        held(rest), u_more, flops=40 << 30,
    )
    return call(
        last_kernel,
        jax.ShapeDtypeStruct((LANES, rows), BF16),
        mine,
        lax.ppermute(to_both, ("y", "zl"), far_z),
        lax.ppermute(to_far, "y", far),
        lax.ppermute(to_z, "zl", cores),
        v_all.reshape(v_shape),
        scratch=[pltpu.VMEM(flat, F32)],
    )


def solution(mesh):
    axes = ("x", "zh", "y", "zl", "c")
    fine = Mesh(mesh.devices.reshape(4, 2, 4, 2, 2), axes)
    pair, ctr = ("x", "zh"), ("y", "zl", "c")
    in_specs = (P(pair, ctr), P(ctr, None), P(ctr, None), P(), P(ctr), P())
    return jax.shard_map(body, mesh=fine, in_specs=in_specs, out_specs=P(ctr, pair), check_vma=False)
```

```python
import functools

import jax
import jax.numpy as jnp
from jax import lax
from jax.experimental import pallas as pl
from jax.experimental.pallas import tpu as pltpu
from jax.sharding import Mesh, PartitionSpec as P

F32, BF16, I32, I16 = jnp.float32, jnp.bfloat16, jnp.int32, jnp.int16
LANES = 128
MIB = 1 << 20
VMEM = pl.BlockSpec(memory_space=pltpu.VMEM)
HBM = pl.BlockSpec(memory_space=pltpu.HBM)


def across(column, width):
    return jnp.broadcast_to(column, (column.shape[0], width))


def mask_rows(me, occ_ref, map_ref, col_ref, t_ref, tm_ref, label_ref):
    orbitals = occ_ref.shape[1]
    rows, depth = t_ref.shape
    own = rows // orbitals
    irreps = map_ref.shape[0]
    square = (orbitals, orbitals)
    diagonal = lax.broadcasted_iota(I32, square, 0) == lax.broadcasted_iota(I32, square, 1)
    labels = jnp.where(diagonal, jnp.broadcast_to(occ_ref[...], square), 0)
    label_ref[...] = across(jnp.sum(labels, axis=1, keepdims=True), LANES)
    weights = jnp.left_shift(1, lax.broadcasted_iota(I32, map_ref.shape, 1))
    kept = across(jnp.sum(map_ref[...] * weights, axis=1, keepdims=True), LANES)
    bit = jnp.left_shift(1, jnp.broadcast_to(col_ref[...], (16, depth))).astype(I16)
    bit = jnp.concatenate([bit] * (orbitals // 16), axis=0)
    for a in range(own):
        pair = label_ref[...] ^ label_ref[pl.ds(me * own + a, 1), :]
        word = jnp.zeros_like(pair)
        for r in range(irreps):
            word = jnp.where(pair == r, kept[r : r + 1, :], word)
        word = jnp.concatenate([word.astype(I16)] * (depth // LANES), axis=1)
        part = pl.ds(a * orbitals, orbitals)
        tm_ref[part, :] = jnp.where((word & bit) != 0, t_ref[part, :], jnp.zeros((), BF16))


def by_group(x, shape):
    groups, block, _ = shape
    own = block // groups
    return jnp.swapaxes(x.reshape(own, groups, own, LANES), 0, 1).reshape(shape)


def v_kernel(
    occ_hbm, map_hbm, col_hbm, t_hbm, p_hbm, m_hbm,
    keep_ref, send_ref, tm_ref, p_ref, m_ref,
    occ_ref, map_ref, col_ref, label_ref, t_ref, small_sem, p_sem, m_sem,
):
    slabs = p_ref.shape[0]
    groups, _, block, _ = keep_ref.shape
    wide = 2 * LANES
    me = lax.axis_index("x") * lax.axis_size("zh") + lax.axis_index("zh")
    core = lax.axis_index("c")
    small = [
        pltpu.make_async_copy(src, dst, small_sem.at[i])
        for i, (src, dst) in enumerate(((t_hbm, t_ref), (occ_hbm, occ_ref), (map_hbm, map_ref), (col_hbm, col_ref)))
    ]
    for copy in small:
        copy.start()

    def loads(s):
        columns = pl.ds(pl.multiple_of(s * wide, wide), wide)
        return (
            pltpu.make_async_copy(p_hbm.at[:, columns], p_ref.at[s], p_sem.at[s]),
            pltpu.make_async_copy(m_hbm.at[:, columns], m_ref.at[s], m_sem.at[s]),
        )

    def start(s, carry):
        for copy in loads(s):
            copy.start()
        return carry

    lax.fori_loop(0, slabs, start, 0)
    for copy in small:
        copy.wait()
    mask_rows(me, occ_ref, map_ref, col_ref, t_ref, tm_ref, label_ref)
    shape = (groups, block, LANES)

    def step(b, carry):
        weights = []
        for i in range(2):
            for copy in loads(2 * b + i):
                copy.wait()
            weights.append(p_ref[2 * b + i] - m_ref[2 * b + i])
        v = jnp.dot(tm_ref[...], jnp.concatenate(weights, axis=1), preferred_element_type=F32)
        for i in range(2):
            low = v[:, 2 * i * LANES : (2 * i + 1) * LANES]
            high = v[:, (2 * i + 1) * LANES : (2 * i + 2) * LANES]
            keep_ref[:, 2 * b + i] = by_group(jnp.where(core == 0, low, high), shape)
            send_ref[:, 2 * b + i] = by_group(jnp.where(core == 0, high, low), shape).astype(BF16)
        return carry

    lax.fori_loop(0, slabs // 2, step, 0)


def u_kernel(parity, unroll, tm_ref, p_ref, m_ref, out_ref):
    y, zl = lax.axis_index("y"), lax.axis_index("zl")
    columns = pl.ds(pl.multiple_of(parity * LANES, LANES), LANES)
    near, far = y ^ 1, 3 - y

    def step(b, carry):
        weights = [p_ref[4 * b + i, :, columns] + m_ref[4 * b + i, :, columns] for i in range(4)]
        u = jnp.dot(tm_ref[...], jnp.concatenate(weights, axis=1), preferred_element_type=F32)
        for i in range(4):
            s = 4 * b + i
            ys, zs = s // 2, s % 2
            z_slot = jnp.where(zs == zl, 0, 1)
            y_slot = jnp.where(ys == y, 0, jnp.where(ys == far, 1, jnp.where(ys == near, 2, 3)))
            out_ref[y_slot, z_slot] = u[:, i * LANES : (i + 1) * LANES].astype(out_ref.dtype)
        return carry

    lax.fori_loop(0, p_ref.shape[0] // 4, step, 0, unroll=unroll)


def u_send_kernel(*refs):
    u_kernel(1 - lax.axis_index("c"), True, *refs)


def u_keep_kernel(tm_ref, p_ref, m_ref, vk_ref, vg_ref, out_ref, v_hbm, v_ref, sem):
    copies = []
    for h in range(v_ref.shape[0]):
        v_ref[h] = (vk_ref[h] + vg_ref[h].astype(F32)).astype(BF16)
        copies.append(pltpu.make_async_copy(v_ref.at[h], v_hbm.at[h], sem.at[h]))
        copies[-1].start()
    u_kernel(lax.axis_index("c"), False, tm_ref, p_ref, m_ref, out_ref)
    for copy in copies:
        copy.wait()


def first_add_kernel(keep_ref, got_ref, out_ref, rest_ref):
    for slot in range(2):
        for z in range(2):
            total = keep_ref[2 + slot, z] + got_ref[2 + slot, z].astype(F32)
            out_ref[slot, z] = total.astype(BF16)
            rest_ref[slot, z] = keep_ref[slot, z] + got_ref[slot, z].astype(F32)


def second_add_kernel(rest_ref, more_ref, mine_ref, *out_refs):
    for ref, (slot, z) in zip((mine_ref, *out_refs), ((0, 0), (1, 1), (1, 0), (0, 1))):
        ref[...] = (rest_ref[slot, z] + more_ref[slot, z].astype(F32)).astype(ref.dtype)


def v_sum_kernel(v_ref, out_ref, scratch):
    groups, slabs, block, _ = v_ref.shape
    own = block // groups
    for g in range(groups):
        v = v_ref[g, 0].astype(F32)
        for s in range(1, slabs):
            v = v + v_ref[g, s].astype(F32)
        scratch[pl.ds(g * block, block), :] = v
    orbitals = groups * own
    for b in range(own):
        out_ref[pl.ds(b * orbitals, orbitals), :] = scratch[pl.ds(b, orbitals, stride=own), :]


def last_kernel(mine_ref, both_ref, far_ref, z_ref, v_ref, out_ref):
    total = mine_ref[...] + v_ref[...]
    for ref in (both_ref, far_ref, z_ref):
        total = total + ref[...].astype(F32)
    out_ref[...] = (0.5 * total).T.astype(BF16)


def held(x):
    return pltpu.with_memory_space_constraint(x, pltpu.VMEM)


def call(kernel, out_shape, *operands, flops=MIB, scratch=()):
    return pl.pallas_call(
        kernel,
        in_specs=[VMEM] * len(operands),
        out_specs=jax.tree.map(lambda _: VMEM, out_shape),
        out_shape=out_shape,
        scratch_shapes=scratch,
        compiler_params=pltpu.CompilerParams(vmem_limit_bytes=8 * MIB),
        cost_estimate=pl.CostEstimate(flops=flops, bytes_accessed=4 * MIB, transcendentals=0),
    )(*operands)


def body(amplitudes, v_plus, v_minus, occ_irrep, col_irrep, block_map):
    rows, depth = amplitudes.shape
    width = v_plus.shape[1]
    orbitals = occ_irrep.shape[0]
    groups = lax.axis_size("x") * lax.axis_size("zh")
    ys, zs = lax.axis_size("y"), lax.axis_size("zl")
    slabs = ys * zs
    block = rows // groups
    operands = (occ_irrep.reshape(1, orbitals), block_map, col_irrep.reshape(1, depth), amplitudes, v_plus, v_minus)
    v_shape, u_shape = (groups, slabs, block, LANES), (ys, zs, rows, LANES)
    wide = (slabs, depth, 2 * LANES)
    flops = rows * depth * width
    v_keep, v_send, tm, p, m = pl.pallas_call(
        v_kernel,
        in_specs=[HBM] * 6,
        out_specs=[VMEM] * 5,
        out_shape=[
            pltpu.VMEM(v_shape, F32),
            pltpu.VMEM(v_shape, BF16),
            pltpu.VMEM((rows, depth), BF16),
            pltpu.VMEM(wide, BF16),
            pltpu.VMEM(wide, BF16),
        ],
        scratch_shapes=[
            pltpu.VMEM((1, orbitals), I32),
            pltpu.VMEM(block_map.shape, I32),
            pltpu.VMEM((1, depth), I32),
            pltpu.VMEM((orbitals, LANES), I32),
            pltpu.VMEM((rows, depth), BF16),
            pltpu.SemaphoreType.DMA((4,)),
            pltpu.SemaphoreType.DMA((slabs,)),
            pltpu.SemaphoreType.DMA((slabs,)),
        ],
        compiler_params=pltpu.CompilerParams(vmem_limit_bytes=12 * MIB),
        cost_estimate=pl.CostEstimate(flops=2 * flops, bytes_accessed=20 * MIB, transcendentals=0),
    )(*(pltpu.with_memory_space_constraint(x, pltpu.HBM) for x in operands))

    def after(x, *others):
        return lax.optimization_barrier((x, *others))[0]

    cores = [(0, 1), (1, 0)]
    near = [(i, i ^ 1) for i in range(ys)]
    far = [(i, ys - 1 - i) for i in range(ys)]
    far_z = [(2 * a + z, 2 * b + 1 - z) for a, b in far for z in range(2)]
    flat = (rows, LANES)
    v_got = lax.ppermute(v_send, "c", cores)
    factors = [held(x) for x in (tm, p, m)]
    u_send = call(u_send_kernel, pltpu.VMEM(u_shape, BF16), *factors, flops=flops)
    u_got = lax.ppermute(u_send, "c", cores)
    u_keep, v_part = pl.pallas_call(
        u_keep_kernel,
        in_specs=[VMEM] * 5,
        out_specs=[VMEM, HBM],
        out_shape=[pltpu.VMEM(u_shape, F32), pltpu.HBM(v_shape, BF16)],
        scratch_shapes=[pltpu.VMEM(v_shape, BF16), pltpu.SemaphoreType.DMA((groups,))],
        compiler_params=pltpu.CompilerParams(vmem_limit_bytes=8 * MIB),
        cost_estimate=pl.CostEstimate(flops=flops, bytes_accessed=4 * MIB, transcendentals=0),
    )(*factors, held(after(v_keep, u_send)), held(v_got))
    u_out, rest = call(
        first_add_kernel,
        [jax.ShapeDtypeStruct((2, zs, *flat), BF16), pltpu.VMEM((2, zs, *flat), F32)],
        held(u_keep), held(u_got),
    )
    u_more = lax.ppermute(u_out, "y", near)
    v_part = after(v_part, rest)
    v_all = lax.all_to_all(
        v_part.reshape(groups * slabs, block, LANES), ("x", "zh", "y", "zl"), 0, 0, tiled=True
    )
    mine, to_both, to_far, to_z = call(
        second_add_kernel,
        [pltpu.VMEM(flat, F32)] + [jax.ShapeDtypeStruct(flat, BF16)] * 3,
        held(rest), u_more, flops=40 << 30,
    )
    v_sum = call(
        v_sum_kernel, pltpu.VMEM(flat, F32), v_all.reshape(v_shape), flops=4 << 30, scratch=[pltpu.VMEM(flat, F32)]
    )
    return call(
        last_kernel,
        jax.ShapeDtypeStruct((LANES, rows), BF16),
        held(mine),
        lax.ppermute(to_both, ("y", "zl"), far_z),
        lax.ppermute(to_far, "y", far),
        lax.ppermute(to_z, "zl", cores),
        held(v_sum),
    )


def solution(mesh):
    axes = ("x", "zh", "y", "zl", "c")
    fine = Mesh(mesh.devices.reshape(4, 2, 4, 2, 2), axes)
    pair, ctr = ("x", "zh"), ("y", "zl", "c")
    in_specs = (P(pair, ctr), P(ctr, None), P(ctr, None), P(), P(ctr), P())
    return jax.shard_map(body, mesh=fine, in_specs=in_specs, out_specs=P(ctr, pair), check_vma=False)
```

```python
import functools

import jax
import jax.numpy as jnp
from jax import lax
from jax.experimental import pallas as pl
from jax.experimental.pallas import tpu as pltpu
from jax.sharding import Mesh, PartitionSpec as P

F32, BF16, I32, I16 = jnp.float32, jnp.bfloat16, jnp.int32, jnp.int16
LANES = 128
MIB = 1 << 20
VMEM = pl.BlockSpec(memory_space=pltpu.VMEM)
HBM = pl.BlockSpec(memory_space=pltpu.HBM)


def across(column, width):
    return jnp.broadcast_to(column, (column.shape[0], width))


def mask_rows(me, occ_ref, map_ref, col_ref, t_ref, tm_ref, label_ref):
    orbitals = occ_ref.shape[1]
    rows, depth = t_ref.shape
    own = rows // orbitals
    irreps = map_ref.shape[0]
    square = (orbitals, orbitals)
    diagonal = lax.broadcasted_iota(I32, square, 0) == lax.broadcasted_iota(I32, square, 1)
    labels = jnp.where(diagonal, jnp.broadcast_to(occ_ref[...], square), 0)
    label_ref[...] = across(jnp.sum(labels, axis=1, keepdims=True), LANES)
    weights = jnp.left_shift(1, lax.broadcasted_iota(I32, map_ref.shape, 1))
    kept = across(jnp.sum(map_ref[...] * weights, axis=1, keepdims=True), LANES)
    bit = jnp.left_shift(1, jnp.broadcast_to(col_ref[...], (16, depth))).astype(I16)
    bit = jnp.concatenate([bit] * (orbitals // 16), axis=0)
    for a in range(own):
        pair = label_ref[...] ^ label_ref[pl.ds(me * own + a, 1), :]
        word = jnp.zeros_like(pair)
        for r in range(irreps):
            word = jnp.where(pair == r, kept[r : r + 1, :], word)
        word = jnp.concatenate([word.astype(I16)] * (depth // LANES), axis=1)
        part = pl.ds(a * orbitals, orbitals)
        tm_ref[part, :] = jnp.where((word & bit) != 0, t_ref[part, :], jnp.zeros((), BF16))


def by_group(x, shape):
    groups, block, _ = shape
    own = block // groups
    return jnp.swapaxes(x.reshape(own, groups, own, LANES), 0, 1).reshape(shape)


def slot_of(s):
    y, zl = lax.axis_index("y"), lax.axis_index("zl")
    ys, zs = s // 2, s % 2
    near, far = y ^ 1, 3 - y
    y_slot = jnp.where(ys == y, 0, jnp.where(ys == far, 1, jnp.where(ys == near, 2, 3)))
    return y_slot, jnp.where(zs == zl, 0, 1)


def send_kernel(
    occ_hbm, map_hbm, col_hbm, t_hbm, p_hbm, m_hbm,
    vs_ref, us_ref, tm_ref, p_ref, m_ref,
    occ_ref, map_ref, col_ref, label_ref, t_ref, small_sem, p_sem, m_sem,
):
    slabs = p_ref.shape[0]
    groups, _, block, _ = vs_ref.shape
    wide = 2 * LANES
    me = lax.axis_index("x") * lax.axis_size("zh") + lax.axis_index("zh")
    core = lax.axis_index("c")
    small = [
        pltpu.make_async_copy(src, dst, small_sem.at[i])
        for i, (src, dst) in enumerate(((t_hbm, t_ref), (occ_hbm, occ_ref), (map_hbm, map_ref), (col_hbm, col_ref)))
    ]
    for copy in small:
        copy.start()

    def loads(s):
        columns = pl.ds(pl.multiple_of(s * wide, wide), wide)
        return (
            pltpu.make_async_copy(p_hbm.at[:, columns], p_ref.at[s], p_sem.at[s]),
            pltpu.make_async_copy(m_hbm.at[:, columns], m_ref.at[s], m_sem.at[s]),
        )

    def start(s, carry):
        for copy in loads(s):
            copy.start()
        return carry

    lax.fori_loop(0, slabs, start, 0)
    for copy in small:
        copy.wait()
    mask_rows(me, occ_ref, map_ref, col_ref, t_ref, tm_ref, label_ref)
    shape = (groups, block, LANES)

    other = pl.ds(pl.multiple_of((1 - core) * LANES, LANES), LANES)

    def step(b, carry):
        less, more = [], []
        for i in range(2):
            for copy in loads(2 * b + i):
                copy.wait()
            left, right = p_ref[2 * b + i, :, other], m_ref[2 * b + i, :, other]
            less.append(left - right)
            more.append(left + right)
        both = jnp.dot(tm_ref[...], jnp.concatenate(less + more, axis=1), preferred_element_type=F32)
        for i in range(2):
            vs_ref[:, 2 * b + i] = by_group(both[:, i * LANES : (i + 1) * LANES], shape).astype(BF16)
            y_slot, z_slot = slot_of(2 * b + i)
            us_ref[y_slot, z_slot] = both[:, (2 + i) * LANES : (3 + i) * LANES].astype(BF16)
        return carry

    lax.fori_loop(0, slabs // 2, step, 0)


def u_kernel(tm_ref, p_ref, m_ref, out_ref):
    columns = pl.ds(pl.multiple_of(lax.axis_index("c") * LANES, LANES), LANES)

    def step(b, carry):
        weights = [p_ref[4 * b + i, :, columns] + m_ref[4 * b + i, :, columns] for i in range(4)]
        u = jnp.dot(tm_ref[...], jnp.concatenate(weights, axis=1), preferred_element_type=F32)
        for i in range(4):
            y_slot, z_slot = slot_of(4 * b + i)
            out_ref[y_slot, z_slot] = u[:, i * LANES : (i + 1) * LANES]
        return carry

    lax.fori_loop(0, p_ref.shape[0] // 4, step, 0, unroll=True)


def v_kernel(tm_ref, p_ref, m_ref, got_ref, out_hbm, out_ref, sem):
    groups, slabs, block, _ = out_ref.shape
    columns = pl.ds(pl.multiple_of(lax.axis_index("c") * LANES, LANES), LANES)
    copies = []
    for b in range(slabs // 4):
        weights = [p_ref[4 * b + i, :, columns] - m_ref[4 * b + i, :, columns] for i in range(4)]
        v = jnp.dot(tm_ref[...], jnp.concatenate(weights, axis=1), preferred_element_type=F32)
        for i in range(4):
            own = by_group(v[:, i * LANES : (i + 1) * LANES], (groups, block, LANES))
            out_ref[:, 4 * b + i] = (own + got_ref[:, 4 * b + i].astype(F32)).astype(BF16)
        part = pl.ds(4 * b, 4)
        copies.append(pltpu.make_async_copy(out_ref.at[:, part], out_hbm.at[:, part], sem.at[b]))
        copies[-1].start()
    for copy in copies:
        copy.wait()


def first_add_kernel(keep_ref, got_ref, out_ref, rest_ref):
    for slot in range(2):
        for z in range(2):
            total = keep_ref[2 + slot, z] + got_ref[2 + slot, z].astype(F32)
            out_ref[slot, z] = total.astype(BF16)
            rest_ref[slot, z] = keep_ref[slot, z] + got_ref[slot, z].astype(F32)


def second_add_kernel(rest_ref, more_ref, mine_ref, *out_refs):
    for ref, (slot, z) in zip((mine_ref, *out_refs), ((0, 0), (1, 1), (1, 0), (0, 1))):
        ref[...] = (rest_ref[slot, z] + more_ref[slot, z].astype(F32)).astype(ref.dtype)


def v_sum_kernel(v_ref, out_ref, scratch):
    groups, slabs, block, _ = v_ref.shape
    own = block // groups
    for g in range(groups):
        v = v_ref[g, 0].astype(F32)
        for s in range(1, slabs):
            v = v + v_ref[g, s].astype(F32)
        scratch[pl.ds(g * block, block), :] = v
    orbitals = groups * own
    for b in range(own):
        out_ref[pl.ds(b * orbitals, orbitals), :] = scratch[pl.ds(b, orbitals, stride=own), :]


def last_kernel(mine_ref, both_ref, far_ref, z_ref, v_ref, out_ref):
    total = mine_ref[...] + v_ref[...]
    for ref in (both_ref, far_ref, z_ref):
        total = total + ref[...].astype(F32)
    out_ref[...] = (0.5 * total).T.astype(BF16)


def held(x):
    return pltpu.with_memory_space_constraint(x, pltpu.VMEM)


def call(kernel, out_shape, *operands, flops=MIB, scratch=()):
    return pl.pallas_call(
        kernel,
        in_specs=[VMEM] * len(operands),
        out_specs=jax.tree.map(lambda _: VMEM, out_shape),
        out_shape=out_shape,
        scratch_shapes=scratch,
        compiler_params=pltpu.CompilerParams(vmem_limit_bytes=8 * MIB),
        cost_estimate=pl.CostEstimate(flops=flops, bytes_accessed=4 * MIB, transcendentals=0),
    )(*operands)


def body(amplitudes, v_plus, v_minus, occ_irrep, col_irrep, block_map):
    rows, depth = amplitudes.shape
    width = v_plus.shape[1]
    orbitals = occ_irrep.shape[0]
    groups = lax.axis_size("x") * lax.axis_size("zh")
    ys, zs = lax.axis_size("y"), lax.axis_size("zl")
    slabs = ys * zs
    block = rows // groups
    operands = (occ_irrep.reshape(1, orbitals), block_map, col_irrep.reshape(1, depth), amplitudes, v_plus, v_minus)
    v_shape, u_shape = (groups, slabs, block, LANES), (ys, zs, rows, LANES)
    wide = (slabs, depth, 2 * LANES)
    flops = rows * depth * width
    v_send, u_send, tm, p, m = pl.pallas_call(
        send_kernel,
        in_specs=[HBM] * 6,
        out_specs=[VMEM] * 5,
        out_shape=[
            pltpu.VMEM(v_shape, BF16),
            pltpu.VMEM(u_shape, BF16),
            pltpu.VMEM((rows, depth), BF16),
            pltpu.VMEM(wide, BF16),
            pltpu.VMEM(wide, BF16),
        ],
        scratch_shapes=[
            pltpu.VMEM((1, orbitals), I32),
            pltpu.VMEM(block_map.shape, I32),
            pltpu.VMEM((1, depth), I32),
            pltpu.VMEM((orbitals, LANES), I32),
            pltpu.VMEM((rows, depth), BF16),
            pltpu.SemaphoreType.DMA((4,)),
            pltpu.SemaphoreType.DMA((slabs,)),
            pltpu.SemaphoreType.DMA((slabs,)),
        ],
        compiler_params=pltpu.CompilerParams(vmem_limit_bytes=12 * MIB),
        cost_estimate=pl.CostEstimate(flops=2 * flops, bytes_accessed=20 * MIB, transcendentals=0),
    )(*(pltpu.with_memory_space_constraint(x, pltpu.HBM) for x in operands))

    def after(x, *others):
        return lax.optimization_barrier((x, *others))[0]

    cores = [(0, 1), (1, 0)]
    near = [(i, i ^ 1) for i in range(ys)]
    far = [(i, ys - 1 - i) for i in range(ys)]
    far_z = [(2 * a + z, 2 * b + 1 - z) for a, b in far for z in range(2)]
    flat = (rows, LANES)
    factors = [held(x) for x in (p, m)]
    u_got = lax.ppermute(u_send, "c", cores)
    v_got = lax.ppermute(v_send, "c", cores)
    u_keep = call(u_kernel, pltpu.VMEM(u_shape, F32), held(tm), *factors, flops=flops)
    u_out, rest = call(
        first_add_kernel,
        [jax.ShapeDtypeStruct((2, zs, *flat), BF16), pltpu.VMEM((2, zs, *flat), F32)],
        held(u_keep), held(u_got),
    )
    u_more = lax.ppermute(u_out, "y", near)
    v_part = pl.pallas_call(
        v_kernel,
        in_specs=[VMEM] * 4,
        out_specs=HBM,
        out_shape=pltpu.HBM(v_shape, BF16),
        scratch_shapes=[pltpu.VMEM(v_shape, BF16), pltpu.SemaphoreType.DMA((slabs // 4,))],
        compiler_params=pltpu.CompilerParams(vmem_limit_bytes=8 * MIB),
        cost_estimate=pl.CostEstimate(flops=flops, bytes_accessed=4 * MIB, transcendentals=0),
    )(held(after(tm, rest)), *factors, held(v_got))
    v_all = lax.all_to_all(
        v_part.reshape(groups * slabs, block, LANES), ("x", "zh", "y", "zl"), 0, 0, tiled=True
    )
    mine, to_both, to_far, to_z = call(
        second_add_kernel,
        [pltpu.VMEM(flat, F32)] + [jax.ShapeDtypeStruct(flat, BF16)] * 3,
        held(rest), u_more, flops=40 << 30,
    )
    v_sum = call(
        v_sum_kernel, pltpu.VMEM(flat, F32), v_all.reshape(v_shape), flops=4 << 30, scratch=[pltpu.VMEM(flat, F32)]
    )
    return call(
        last_kernel,
        jax.ShapeDtypeStruct((LANES, rows), BF16),
        held(mine),
        lax.ppermute(to_both, ("y", "zl"), far_z),
        lax.ppermute(to_far, "y", far),
        lax.ppermute(to_z, "zl", cores),
        held(v_sum),
    )


def solution(mesh):
    axes = ("x", "zh", "y", "zl", "c")
    fine = Mesh(mesh.devices.reshape(4, 2, 4, 2, 2), axes)
    pair, ctr = ("x", "zh"), ("y", "zl", "c")
    in_specs = (P(pair, ctr), P(ctr, None), P(ctr, None), P(), P(ctr), P())
    return jax.shard_map(body, mesh=fine, in_specs=in_specs, out_specs=P(ctr, pair), check_vma=False)
```

```python
import functools

import jax
import jax.numpy as jnp
from jax import lax
from jax.experimental import pallas as pl
from jax.experimental.pallas import tpu as pltpu
from jax.sharding import Mesh, PartitionSpec as P

F32, BF16, I32, I16 = jnp.float32, jnp.bfloat16, jnp.int32, jnp.int16
LANES = 128
MIB = 1 << 20
VMEM = pl.BlockSpec(memory_space=pltpu.VMEM)
HBM = pl.BlockSpec(memory_space=pltpu.HBM)


def across(column, width):
    return jnp.broadcast_to(column, (column.shape[0], width))


def mask_rows(me, occ_ref, map_ref, col_ref, t_ref, tm_ref, label_ref):
    orbitals = occ_ref.shape[1]
    rows, depth = t_ref.shape
    own = rows // orbitals
    irreps = map_ref.shape[0]
    square = (orbitals, orbitals)
    diagonal = lax.broadcasted_iota(I32, square, 0) == lax.broadcasted_iota(I32, square, 1)
    labels = jnp.where(diagonal, jnp.broadcast_to(occ_ref[...], square), 0)
    label_ref[...] = across(jnp.sum(labels, axis=1, keepdims=True), LANES)
    weights = jnp.left_shift(1, lax.broadcasted_iota(I32, map_ref.shape, 1))
    kept = across(jnp.sum(map_ref[...] * weights, axis=1, keepdims=True), LANES)
    bit = jnp.left_shift(1, jnp.broadcast_to(col_ref[...], (16, depth))).astype(I16)
    bit = jnp.concatenate([bit] * (orbitals // 16), axis=0)
    for a in range(own):
        pair = label_ref[...] ^ label_ref[pl.ds(me * own + a, 1), :]
        word = jnp.zeros_like(pair)
        for r in range(irreps):
            word = jnp.where(pair == r, kept[r : r + 1, :], word)
        word = jnp.concatenate([word.astype(I16)] * (depth // LANES), axis=1)
        part = pl.ds(a * orbitals, orbitals)
        tm_ref[part, :] = jnp.where((word & bit) != 0, t_ref[part, :], jnp.zeros((), BF16))


def by_group(x, shape):
    groups, block, _ = shape
    own = block // groups
    return jnp.swapaxes(x.reshape(own, groups, own, LANES), 0, 1).reshape(shape)


def slot_of(s):
    y, zl = lax.axis_index("y"), lax.axis_index("zl")
    ys, zs = s // 2, s % 2
    near, far = y ^ 1, 3 - y
    y_slot = jnp.where(ys == y, 0, jnp.where(ys == far, 1, jnp.where(ys == near, 2, 3)))
    return y_slot, jnp.where(zs == zl, 0, 1)


def send_kernel(
    occ_hbm, map_hbm, col_hbm, t_hbm, p_hbm, m_hbm,
    vs_ref, us_ref, tm_ref, p_ref, m_ref,
    occ_ref, map_ref, col_ref, label_ref, t_ref, small_sem, p_sem, m_sem,
):
    slabs = p_ref.shape[0]
    groups, _, block, _ = vs_ref.shape
    wide = 2 * LANES
    me = lax.axis_index("x") * lax.axis_size("zh") + lax.axis_index("zh")
    core = lax.axis_index("c")
    small = [
        pltpu.make_async_copy(src, dst, small_sem.at[i])
        for i, (src, dst) in enumerate(((t_hbm, t_ref), (occ_hbm, occ_ref), (map_hbm, map_ref), (col_hbm, col_ref)))
    ]
    for copy in small:
        copy.start()

    def loads(s):
        columns = pl.ds(pl.multiple_of(s * wide, wide), wide)
        return (
            pltpu.make_async_copy(p_hbm.at[:, columns], p_ref.at[s], p_sem.at[s]),
            pltpu.make_async_copy(m_hbm.at[:, columns], m_ref.at[s], m_sem.at[s]),
        )

    def start(s, carry):
        for copy in loads(s):
            copy.start()
        return carry

    lax.fori_loop(0, slabs, start, 0)
    for copy in small:
        copy.wait()
    mask_rows(me, occ_ref, map_ref, col_ref, t_ref, tm_ref, label_ref)
    shape = (groups, block, LANES)

    other = pl.ds(pl.multiple_of((1 - core) * LANES, LANES), LANES)

    def step(b, carry):
        less, more = [], []
        for i in range(2):
            for copy in loads(2 * b + i):
                copy.wait()
            left, right = p_ref[2 * b + i, :, other], m_ref[2 * b + i, :, other]
            less.append(left - right)
            more.append(left + right)
        both = jnp.dot(tm_ref[...], jnp.concatenate(less + more, axis=1), preferred_element_type=F32)
        for i in range(2):
            vs_ref[:, 2 * b + i] = by_group(both[:, i * LANES : (i + 1) * LANES], shape).astype(BF16)
            y_slot, z_slot = slot_of(2 * b + i)
            us_ref[y_slot, z_slot] = both[:, (2 + i) * LANES : (3 + i) * LANES].astype(BF16)
        return carry

    lax.fori_loop(0, slabs // 2, step, 0)


def u_kernel(tm_ref, p_ref, m_ref, out_ref):
    columns = pl.ds(pl.multiple_of(lax.axis_index("c") * LANES, LANES), LANES)

    def step(b, carry):
        weights = [p_ref[4 * b + i, :, columns] + m_ref[4 * b + i, :, columns] for i in range(4)]
        u = jnp.dot(tm_ref[...], jnp.concatenate(weights, axis=1), preferred_element_type=F32)
        for i in range(4):
            y_slot, z_slot = slot_of(4 * b + i)
            out_ref[y_slot, z_slot] = u[:, i * LANES : (i + 1) * LANES]
        return carry

    lax.fori_loop(0, p_ref.shape[0] // 4, step, 0, unroll=True)


def v_kernel(tm_ref, p_ref, m_ref, got_ref, out_hbm, out_ref, sem):
    groups, slabs, block, _ = out_ref.shape
    columns = pl.ds(pl.multiple_of(lax.axis_index("c") * LANES, LANES), LANES)
    copies = []
    for b in range(slabs // 4):
        weights = [p_ref[4 * b + i, :, columns] - m_ref[4 * b + i, :, columns] for i in range(4)]
        v = jnp.dot(tm_ref[...], jnp.concatenate(weights, axis=1), preferred_element_type=F32)
        for i in range(4):
            own = by_group(v[:, i * LANES : (i + 1) * LANES], (groups, block, LANES))
            out_ref[:, 4 * b + i] = (own + got_ref[:, 4 * b + i].astype(F32)).astype(BF16)
        part = pl.ds(4 * b, 4)
        copies.append(pltpu.make_async_copy(out_ref.at[:, part], out_hbm.at[:, part], sem.at[b]))
        copies[-1].start()
    for copy in copies:
        copy.wait()


def first_add_kernel(keep_ref, got_ref, out_ref, rest_ref):
    for slot in range(2):
        for z in range(2):
            total = keep_ref[2 + slot, z] + got_ref[2 + slot, z].astype(F32)
            out_ref[slot, z] = total.astype(BF16)
            rest_ref[slot, z] = keep_ref[slot, z] + got_ref[slot, z].astype(F32)


def second_add_kernel(rest_ref, more_ref, mine_ref, *out_refs):
    for ref, (slot, z) in zip((mine_ref, *out_refs), ((0, 0), (1, 1), (1, 0), (0, 1))):
        ref[...] = (rest_ref[slot, z] + more_ref[slot, z].astype(F32)).astype(ref.dtype)


def v_sum_kernel(v_ref, out_ref, scratch):
    groups, slabs, block, _ = v_ref.shape
    own = block // groups
    for g in range(groups):
        v = v_ref[g, 0].astype(F32)
        for s in range(1, slabs):
            v = v + v_ref[g, s].astype(F32)
        scratch[pl.ds(g * block, block), :] = v
    orbitals = groups * own
    for b in range(own):
        out_ref[pl.ds(b * orbitals, orbitals), :] = scratch[pl.ds(b, orbitals, stride=own), :]


def last_kernel(mine_ref, both_ref, far_ref, z_ref, v_ref, out_hbm, out_ref, sem):
    half = mine_ref.shape[0] // 2
    copies = []
    for i in range(2):
        rows = pl.ds(i * half, half)
        total = mine_ref[rows, :] + v_ref[rows, :]
        for ref in (both_ref, far_ref, z_ref):
            total = total + ref[rows, :].astype(F32)
        out_ref[i] = (0.5 * total).T.astype(BF16)
        copies.append(pltpu.make_async_copy(out_ref.at[i], out_hbm.at[:, rows], sem.at[i]))
        copies[-1].start()
    for copy in copies:
        copy.wait()


def held(x):
    return pltpu.with_memory_space_constraint(x, pltpu.VMEM)


def call(kernel, out_shape, *operands, flops=MIB, scratch=()):
    return pl.pallas_call(
        kernel,
        in_specs=[VMEM] * len(operands),
        out_specs=jax.tree.map(lambda _: VMEM, out_shape),
        out_shape=out_shape,
        scratch_shapes=scratch,
        compiler_params=pltpu.CompilerParams(vmem_limit_bytes=8 * MIB),
        cost_estimate=pl.CostEstimate(flops=flops, bytes_accessed=4 * MIB, transcendentals=0),
    )(*operands)


def body(amplitudes, v_plus, v_minus, occ_irrep, col_irrep, block_map):
    rows, depth = amplitudes.shape
    width = v_plus.shape[1]
    orbitals = occ_irrep.shape[0]
    groups = lax.axis_size("x") * lax.axis_size("zh")
    ys, zs = lax.axis_size("y"), lax.axis_size("zl")
    slabs = ys * zs
    block = rows // groups
    operands = (occ_irrep.reshape(1, orbitals), block_map, col_irrep.reshape(1, depth), amplitudes, v_plus, v_minus)
    v_shape, u_shape = (groups, slabs, block, LANES), (ys, zs, rows, LANES)
    wide = (slabs, depth, 2 * LANES)
    flops = rows * depth * width
    v_send, u_send, tm, p, m = pl.pallas_call(
        send_kernel,
        in_specs=[HBM] * 6,
        out_specs=[VMEM] * 5,
        out_shape=[
            pltpu.VMEM(v_shape, BF16),
            pltpu.VMEM(u_shape, BF16),
            pltpu.VMEM((rows, depth), BF16),
            pltpu.VMEM(wide, BF16),
            pltpu.VMEM(wide, BF16),
        ],
        scratch_shapes=[
            pltpu.VMEM((1, orbitals), I32),
            pltpu.VMEM(block_map.shape, I32),
            pltpu.VMEM((1, depth), I32),
            pltpu.VMEM((orbitals, LANES), I32),
            pltpu.VMEM((rows, depth), BF16),
            pltpu.SemaphoreType.DMA((4,)),
            pltpu.SemaphoreType.DMA((slabs,)),
            pltpu.SemaphoreType.DMA((slabs,)),
        ],
        compiler_params=pltpu.CompilerParams(vmem_limit_bytes=12 * MIB),
        cost_estimate=pl.CostEstimate(flops=2 * flops, bytes_accessed=20 * MIB, transcendentals=0),
    )(*(pltpu.with_memory_space_constraint(x, pltpu.HBM) for x in operands))

    def after(x, *others):
        return lax.optimization_barrier((x, *others))[0]

    cores = [(0, 1), (1, 0)]
    near = [(i, i ^ 1) for i in range(ys)]
    far = [(i, ys - 1 - i) for i in range(ys)]
    far_z = [(2 * a + z, 2 * b + 1 - z) for a, b in far for z in range(2)]
    flat = (rows, LANES)
    factors = [held(x) for x in (p, m)]
    u_got = lax.ppermute(u_send, "c", cores)
    v_got = lax.ppermute(v_send, "c", cores)
    u_keep = call(u_kernel, pltpu.VMEM(u_shape, F32), held(tm), *factors, flops=flops)
    u_out, rest = call(
        first_add_kernel,
        [jax.ShapeDtypeStruct((2, zs, *flat), BF16), pltpu.VMEM((2, zs, *flat), F32)],
        held(u_keep), held(u_got),
    )
    u_more = lax.ppermute(u_out, "y", near)
    v_part = pl.pallas_call(
        v_kernel,
        in_specs=[VMEM] * 4,
        out_specs=HBM,
        out_shape=pltpu.HBM(v_shape, BF16),
        scratch_shapes=[pltpu.VMEM(v_shape, BF16), pltpu.SemaphoreType.DMA((slabs // 4,))],
        compiler_params=pltpu.CompilerParams(vmem_limit_bytes=8 * MIB),
        cost_estimate=pl.CostEstimate(flops=flops, bytes_accessed=4 * MIB, transcendentals=0),
    )(held(after(tm, rest)), *factors, held(v_got))
    v_all = lax.all_to_all(
        v_part.reshape(groups * slabs, block, LANES), ("x", "zh", "y", "zl"), 0, 0, tiled=True
    )
    mine, to_both, to_far, to_z = call(
        second_add_kernel,
        [pltpu.VMEM(flat, F32)] + [jax.ShapeDtypeStruct(flat, BF16)] * 3,
        held(rest), u_more, flops=40 << 30,
    )
    v_sum = call(
        v_sum_kernel, pltpu.VMEM(flat, F32), v_all.reshape(v_shape), flops=4 << 30, scratch=[pltpu.VMEM(flat, F32)]
    )
    return pl.pallas_call(
        last_kernel,
        in_specs=[VMEM] * 5,
        out_specs=HBM,
        out_shape=jax.ShapeDtypeStruct((LANES, rows), BF16),
        scratch_shapes=[pltpu.VMEM((2, LANES, rows // 2), BF16), pltpu.SemaphoreType.DMA((2,))],
        compiler_params=pltpu.CompilerParams(vmem_limit_bytes=8 * MIB),
    )(
        held(mine),
        lax.ppermute(to_both, ("y", "zl"), far_z),
        lax.ppermute(to_far, "y", far),
        lax.ppermute(to_z, "zl", cores),
        held(v_sum),
    )


def solution(mesh):
    axes = ("x", "zh", "y", "zl", "c")
    fine = Mesh(mesh.devices.reshape(4, 2, 4, 2, 2), axes)
    pair, ctr = ("x", "zh"), ("y", "zl", "c")
    in_specs = (P(pair, ctr), P(ctr, None), P(ctr, None), P(), P(ctr), P())
    return jax.shard_map(body, mesh=fine, in_specs=in_specs, out_specs=P(ctr, pair), check_vma=False)
```
